512 devices in a mesh: alpha: 32 (over x, y, core), beta: 16 (over z).
Axes of the slice: x: 4, y: 4, z: 16, core: 2. Of those that a mesh axis runs over, the one named last changes fastest.
Arguments:
- vector: float32 [512, 3072], P('alpha', 'beta'), may hold values from -6 to 6
- integrals: float32 [196, 196], replicated, may hold values from -0.078125 to 0.078125
- alpha_targets: int32 [56, 512], replicated, may hold values from 0 to 511
- alpha_pairs: int32 [56, 512], replicated, may hold values from 0 to 195
- alpha_signs: int32 [56, 512], replicated, may hold values from -1 to 1, as said below
- beta_targets: int32 [56, 3072], replicated, may hold values from 0 to 3071
- beta_pairs: int32 [56, 3072], replicated, may hold values from 0 to 195
- beta_signs: int32 [56, 3072], replicated, may hold values from -1 to 1, as said below
Outputs:
- sigma: float32 [512, 3072], P('alpha', 'beta')
The draws below stay inside these ranges and needn't reach their ends.
Inputs may be any that keep to these rules, and one draw needn't show every extreme that they name: `alpha_signs`: every entry is -1 or 1. `beta_signs`: every entry is -1 or 1.
All inputs are finite; a program needn't handle non-finite values.
Results may differ from the reference program's by a relative error of at most 0.0001.
Values sent between devices are 32-bit elements; how exact they have to be, the bound alone decides.
A program may use at most 64 MiB of HBM per device.

```python
import math
import jax
import jax.numpy as jnp
from jax import lax

EXC = 56
PAIRS = 196
NA = 512
NB = 3072


def draw_alpha_signs(key, part):
    return 2 * jax.random.randint(jax.random.fold_in(key, 11), (EXC, NA), 0, 2, dtype=jnp.int32) - 1


def draw_beta_signs(key, part):
    return 2 * jax.random.randint(jax.random.fold_in(key, 23), (EXC, NB), 0, 2, dtype=jnp.int32) - 1


def with_ends(entries, key, low, top_value):
    longest = entries.shape.index(max(entries.shape))
    spots = []
    for shift in (0, 1):
        where = [jax.random.randint(jax.random.fold_in(key, axis), (), 0, length) for axis, length in enumerate(entries.shape)]
        where[longest] = (where[longest] + shift) % entries.shape[longest]
        spots.append(tuple(where))
    return entries.at[spots[0]].set(low).at[spots[1]].set(top_value)


def shard_levels(key, dims, cuts, smallest, top_value):
    factor_of = 1.0
    for dim, parts in cuts:
        draws = jax.random.uniform(jax.random.fold_in(jax.random.fold_in(key, 6), dim), (parts,), jnp.float32, smallest / len(cuts), top_value / len(cuts))
        factor_of = factor_of * jnp.repeat(jnp.exp(draws), dims[dim] // parts).reshape((-1,) + (1,) * (len(dims) - 1 - dim))
    return factor_of


def centred(own_key, extent, width, limit, shards=(), kind=jnp.bfloat16):
    drawn = jax.random.normal(own_key, extent, jnp.float32) * width
    if len(shards) > 0:
        drawn = shard_levels(own_key, extent, shards, -0.22, 0.18) * drawn
    return jnp.clip(drawn, min=-limit, max=limit).astype(kind)


def setup_inputs(seed: int = 0) -> dict:
    streams_of = jax.random.split(jax.random.key(seed), 9)
    vector = centred(streams_of[0], (NA, NB), 1.0, 6.0, ((0, 32), (1, 16)), jnp.float32)
    integrals = centred(streams_of[1], (PAIRS, PAIRS), (2 * EXC * EXC) ** -0.5, 0.078125, (), jnp.float32)
    alpha_targets = with_ends(jax.random.randint(streams_of[2], (EXC, NA), 0, NA), jax.random.fold_in(streams_of[2], 1), 0, NA - 1).astype(jnp.int32)
    alpha_pairs = with_ends(jax.random.randint(streams_of[3], (EXC, NA), 0, PAIRS), jax.random.fold_in(streams_of[3], 1), 0, PAIRS - 1).astype(jnp.int32)
    alpha_signs = draw_alpha_signs(jax.random.fold_in(streams_of[8], 71), 0)
    beta_targets = with_ends(jax.random.randint(streams_of[5], (EXC, NB), 0, NB), jax.random.fold_in(streams_of[5], 1), 0, NB - 1).astype(jnp.int32)
    beta_pairs = with_ends(jax.random.randint(streams_of[6], (EXC, NB), 0, PAIRS), jax.random.fold_in(streams_of[6], 1), 0, PAIRS - 1).astype(jnp.int32)
    beta_signs = draw_beta_signs(jax.random.fold_in(streams_of[8], 71), 0)
    return dict(vector=vector, integrals=integrals, alpha_targets=alpha_targets, alpha_pairs=alpha_pairs, alpha_signs=alpha_signs, beta_targets=beta_targets, beta_pairs=beta_pairs, beta_signs=beta_signs)


def spin_sum(lookup, targets, pairs, signs, integrals):
    col_count = lookup.shape[0]
    strings = targets.shape[0]
    excite = targets.shape[1]
    pair_count = integrals.shape[0]
    block_size = math.gcd(strings, 64)
    block_count = strings // block_size
    string_index = jnp.broadcast_to(jnp.arange(block_size, dtype=jnp.int32)[:, None], (block_size, excite))

    def one_block(collected, block_lists):
        block_targets, block_pairs, block_signs = block_lists
        flat_targets = block_targets.reshape(-1)
        fetched = jnp.take(lookup, flat_targets, axis=1).reshape(col_count, block_size, excite)
        phases = block_signs.astype(lookup.dtype)
        density = jnp.zeros((col_count, block_size, pair_count), lookup.dtype)
        density = density.at[:, string_index, block_pairs].add(fetched * phases[None])
        contracted = jnp.einsum("wsp,qp->wsq", density, integrals, precision=lax.Precision.HIGHEST)
        picked = contracted[:, string_index, block_pairs] * phases[None]
        collected = collected.at[:, flat_targets].add(picked.reshape(col_count, block_size * excite))
        return collected, None

    block_lists = (targets.reshape(block_count, block_size, excite),
                   pairs.reshape(block_count, block_size, excite),
                   signs.reshape(block_count, block_size, excite))
    start_value = jnp.zeros((col_count, lookup.shape[1]), lookup.dtype)
    collected, _ = lax.scan(one_block, start_value, block_lists)
    return collected


def reference(vector, integrals, alpha_targets, alpha_pairs, alpha_signs, beta_targets, beta_pairs, beta_signs):
    alpha_part = spin_sum(vector.T, alpha_targets.T, alpha_pairs.T, alpha_signs.T, integrals).T
    beta_part = spin_sum(vector, beta_targets.T, beta_pairs.T, beta_signs.T, integrals)
    return alpha_part + beta_part
```

```python
import functools

import jax
import jax.numpy as jnp
from jax import lax
from jax.experimental import pallas as pl
from jax.experimental.pallas import tpu as pltpu
from jax.sharding import PartitionSpec as P

MESH = pl.DeviceIdType.MESH
F32, BF16, I32 = jnp.float32, jnp.bfloat16, jnp.int32

EXC, PAIRS = 56, 196
NALPHA, NBETA = 32, 16
ROWS, COLS = 16, 192
HIGH, LOW = 12, 256
STEPS, PER_STEP = 12, 8


def dot(a, b):
    return lax.dot_general(a, b, (((1,), (0,)), ((), ())), preferred_element_type=F32)


def dot_t(a, b):
    return lax.dot_general(a, b, (((1,), (1,)), ((), ())), preferred_element_type=F32)


def split(x):
    high = x.astype(BF16)
    return high, (x - high.astype(F32)).astype(BF16)


def iota(shape, dim):
    return lax.broadcasted_iota(I32, shape, dim)


def codes_of(targets, pairs, signs):
    return targets * 512 + pairs * 2 + (signs > 0).astype(I32)


def stack_halves(first, second):
    pad = jnp.zeros((64 - EXC, 128), I32)
    return jnp.concatenate([first, pad, second, pad], axis=0)


def transposed(codes):
    return jnp.transpose(codes.astype(F32)).astype(I32)


def sign_of(codes, entry):
    return jnp.where((entry & 63) < EXC, ((codes & 1) * 2 - 1).astype(F32), 0.0)


def kernel(
    v_ref, m_ref, at_ref, ap_ref, as_ref, bt_ref, bp_ref, bs_ref,
    out_ref,
    alists, blists, list_sem, mpad, mh, ml,
    ga, gz, za, zsplit,
    low_rows, high_rows, pair_rows, sign_rows,
    acol, arow, asum, oh, acc,
    ra_out, ra_in, rz_out, rz_in,
    sa_sem, ga_sem, sz_sem, gz_sem, sra_sem, ra_sem, srz_sem, rz_sem,
):
    a, b = lax.axis_index("alpha"), lax.axis_index("beta")

    def alpha_peer(d):
        return lax.rem(a + d, NALPHA)

    def beta_peer(d):
        return lax.rem(b + d, NBETA)

    def alpha_copy(src, dst, send, recv, d):
        return pltpu.make_async_remote_copy(
            src_ref=src, dst_ref=dst, send_sem=send.at[d], recv_sem=recv.at[d],
            device_id=(alpha_peer(d), b), device_id_type=MESH)

    def beta_copy(src, dst, send, recv, d):
        return pltpu.make_async_remote_copy(
            src_ref=src, dst_ref=dst, send_sem=send.at[d], recv_sem=recv.at[d],
            device_id=(a, beta_peer(d)), device_id_type=MESH)

    awin = pl.multiple_of((a // 8) * 128, 128)
    bwin = pl.multiple_of((b // 2) * 384, 128)
    list_copies = []
    for i, ref in enumerate((at_ref, ap_ref, as_ref)):
        list_copies.append(pltpu.make_async_copy(
            ref.at[:, pl.ds(awin, 128)], alists.at[i], list_sem.at[i]))
    for i, ref in enumerate((bt_ref, bp_ref, bs_ref)):
        list_copies.append(pltpu.make_async_copy(
            ref.at[:, pl.ds(bwin, 384)], blists.at[i], list_sem.at[3 + i]))
    for copy in list_copies:
        copy.start()

    barrier = pltpu.get_barrier_semaphore()

    @pl.loop(1, NALPHA)
    def _(d):
        pl.semaphore_signal(barrier, inc=1, device_id=(alpha_peer(d), b), device_id_type=MESH)

    @pl.loop(1, NBETA)
    def _(d):
        pl.semaphore_signal(barrier, inc=1, device_id=(a, beta_peer(d)), device_id_type=MESH)

    pl.semaphore_wait(barrier, NALPHA + NBETA - 2)

    @pl.loop(1, NBETA)
    def _(d):
        beta_copy(v_ref, gz.at[b], sz_sem, gz_sem, d).start()

    @pl.loop(1, NALPHA)
    def _(d):
        alpha_copy(v_ref, ga.at[a], sa_sem, ga_sem, d).start()

    gz[b] = v_ref[...]
    ga[a] = v_ref[...]
    mpad[...] = jnp.zeros_like(mpad)
    mpad[0:PAIRS, 0:PAIRS] = m_ref[...]
    high, low = split(mpad[...])
    mh[...] = high
    ml[...] = low
    for copy in list_copies:
        copy.wait()

    code = codes_of(alists[0], alists[1], alists[2])
    shift = lax.rem(a, 8) * 16
    first = pltpu.roll(code, lax.rem(128 - shift, 128), 1)
    second = pltpu.roll(code, lax.rem(248 - shift, 128), 1)
    code = stack_halves(first, second)
    acol[...] = code
    arow[...] = transposed(code)

    code = codes_of(blists[0], blists[1], blists[2])
    odd = lax.rem(b, 2) == 1
    first = jnp.where(odd, pltpu.roll(code, 192, 1)[:, :128], code[:, :128])
    second = jnp.where(odd, pltpu.roll(code, 96, 1)[:, :128], pltpu.roll(code, 288, 1)[:, :128])
    code = transposed(stack_halves(first, second))
    sign_rows[...] = sign_of(code, iota((128, 128), 1))
    pair_rows[...] = (code >> 1) & 255
    low_rows[...] = (code >> 9) & 255
    high_rows[...] = code >> 17

    @pl.loop(1, NALPHA)
    def _(d):
        alpha_copy(v_ref, ga.at[a], sa_sem, ga_sem, d).wait_recv()

    vh, vl = split(ga[...].reshape(NALPHA * ROWS, COLS))
    same = (iota((256, 256), 0) >> 6) == (iota((256, 256), 1) >> 6)
    sigma = None
    for g in range(4):
        oh_c, w_c, oh_r, w_r = [], [], [], []
        for k in (2 * g, 2 * g + 1):
            col = acol[:, k:k + 1]
            oh_c.append(jnp.where((col >> 9) == iota((128, 512), 1), 1.0, 0.0).astype(BF16))
            w_c.append(jnp.where(
                ((col >> 1) & 255) == iota((128, 256), 1), sign_of(col, iota((128, 1), 0)), 0.0
            ).astype(BF16))
            row = arow[k:k + 1, :]
            oh_r.append(jnp.where((row >> 9) == iota((512, 128), 0), 1.0, 0.0).astype(BF16))
            w_r.append(jnp.where(
                ((row >> 1) & 255) == iota((256, 128), 0), sign_of(row, iota((1, 128), 1)), 0.0
            ).astype(BF16))
        oh_c, w_c = jnp.concatenate(oh_c, 0), jnp.concatenate(w_c, 0)
        oh_r, w_r = jnp.concatenate(oh_r, 1), jnp.concatenate(w_r, 1)
        fh, fl = dot(oh_c, vh).astype(BF16), dot(oh_c, vl).astype(BF16)
        uh, ul = dot(w_c, mh[...]).astype(BF16), dot(w_c, ml[...]).astype(BF16)
        kh = jnp.where(same, dot(uh, w_r), 0.0).astype(BF16)
        kl = jnp.where(same, dot(ul, w_r), 0.0).astype(BF16)
        rh, rl = split(dot(kh, fh) + dot(kh, fl) + dot(kl, fh))
        part = dot(oh_r, rh) + dot(oh_r, rl)
        if g == 0:
            asum[...] = part
        else:
            asum[...] += part
    ra_out[...] = asum[...].reshape(NALPHA, ROWS, COLS)

    @pl.loop(1, NALPHA)
    def _(d):
        alpha_copy(ra_out.at[alpha_peer(d)], ra_in.at[a], sra_sem, ra_sem, d).start()

    @pl.loop(1, NBETA)
    def _(d):
        beta_copy(v_ref, gz.at[b], sz_sem, gz_sem, d).wait_recv()

    for i in range(NBETA):
        za[:, COLS * i:COLS * (i + 1)] = gz[i]
    for h in range(HIGH):
        high, low = split(za[:, LOW * h:LOW * (h + 1)])
        zsplit[32 * h:32 * h + 16, :] = high
        zsplit[32 * h + 16:32 * h + 32, :] = low
    acc[...] = jnp.zeros_like(acc)

    quarter = iota((1, 256), 1) >> 6

    @pl.loop(0, STEPS)
    def _(step):
        k0 = pl.multiple_of(step * PER_STEP, PER_STEP)
        lows, highs = low_rows[pl.ds(k0, PER_STEP), :], high_rows[pl.ds(k0, PER_STEP), :]
        pairs, signs = pair_rows[pl.ds(k0, PER_STEP), :], sign_rows[pl.ds(k0, PER_STEP), :]

        def row(x, g):
            return jnp.concatenate([x[2 * g:2 * g + 1, :], x[2 * g + 1:2 * g + 2, :]], axis=1)

        wts, d_high, d_low = [], [], []
        for g in range(4):
            one = jnp.where(row(lows, g) == iota((256, 256), 0), 1.0, 0.0).astype(BF16)
            oh[:, 256 * g:256 * (g + 1)] = one
            picked = dot(zsplit[...], one)
            hrow = row(highs, g)
            f = picked[0:32]
            for h in range(1, HIGH):
                f = jnp.where(hrow == h, picked[32 * h:32 * h + 32], f)
            wt = jnp.where(row(pairs, g) == iota((256, 256), 0), row(signs, g), 0.0).astype(BF16)
            wts.append(wt)
            lhs = jnp.concatenate(
                [jnp.where(quarter == j, f, 0.0).astype(BF16) for j in range(4)], axis=0)
            density = dot_t(lhs, wt)
            for j in range(4):
                dh, dl = split(density[32 * j:32 * j + 16] + density[32 * j + 16:32 * j + 32])
                d_high.append(dh)
                d_low.append(dl)
        d_high, d_low = jnp.concatenate(d_high, 0), jnp.concatenate(d_low, 0)
        image = dot_t(d_high, mh[...]) + dot_t(d_low, mh[...]) + dot_t(d_high, ml[...])
        ih, il = split(image)
        lhs = []
        for g in range(4):
            back = dot(jnp.concatenate([ih[64 * g:64 * g + 64], il[64 * g:64 * g + 64]], 0), wts[g])
            back = back[0:64] + back[64:128]
            r = back[0:16]
            for j in range(1, 4):
                r = jnp.where(quarter == j, back[16 * j:16 * j + 16], r)
            rh = r.astype(BF16).astype(F32)
            r2 = jnp.concatenate([rh, r - rh], 0)
            hrow = row(highs, g)
            lhs.append(jnp.concatenate(
                [jnp.where(hrow == h, r2, 0.0).astype(BF16) for h in range(HIGH)], axis=0))
        acc[...] += dot_t(jnp.concatenate(lhs, 1), oh[...])

    for h in range(HIGH):
        za[:, LOW * h:LOW * (h + 1)] = acc[32 * h:32 * h + 16, :] + acc[32 * h + 16:32 * h + 32, :]
    for i in range(NBETA):
        rz_out[i] = za[:, COLS * i:COLS * (i + 1)]

    @pl.loop(1, NBETA)
    def _(d):
        beta_copy(rz_out.at[beta_peer(d)], rz_in.at[b], srz_sem, rz_sem, d).start()

    ra_in[a] = ra_out[a]
    rz_in[b] = rz_out[b]

    @pl.loop(1, NALPHA)
    def _(d):
        alpha_copy(v_ref, ga.at[a], sa_sem, ga_sem, d).wait_send()
        alpha_copy(ra_out.at[alpha_peer(d)], ra_in.at[a], sra_sem, ra_sem, d).wait()

    total = ra_in[0]
    for i in range(1, NALPHA):
        total = total + ra_in[i]

    @pl.loop(1, NBETA)
    def _(d):
        beta_copy(v_ref, gz.at[b], sz_sem, gz_sem, d).wait_send()
        beta_copy(rz_out.at[beta_peer(d)], rz_in.at[b], srz_sem, rz_sem, d).wait()

    for i in range(NBETA):
        total = total + rz_in[i]
    out_ref[...] = total


def local(vector, integrals, *lists):
    vmem = pl.BlockSpec(memory_space=pltpu.VMEM)
    hbm = pl.BlockSpec(memory_space=pl.ANY)
    dma = pltpu.SemaphoreType.DMA
    return pl.pallas_call(
        kernel,
        out_shape=jax.ShapeDtypeStruct((ROWS, COLS), F32),
        in_specs=[vmem, vmem] + [hbm] * 6,
        out_specs=vmem,
        scratch_shapes=[
            pltpu.VMEM((3, EXC, 128), I32),
            pltpu.VMEM((3, EXC, 384), I32),
            dma((6,)),
            pltpu.VMEM((256, 256), F32),
            pltpu.VMEM((256, 256), BF16),
            pltpu.VMEM((256, 256), BF16),
            pltpu.VMEM((NALPHA, ROWS, COLS), F32),
            pltpu.VMEM((NBETA, ROWS, COLS), F32),
            pltpu.VMEM((ROWS, NBETA * COLS), F32),
            pltpu.VMEM((2 * HIGH * ROWS, LOW), BF16),
            pltpu.VMEM((128, 128), I32),
            pltpu.VMEM((128, 128), I32),
            pltpu.VMEM((128, 128), I32),
            pltpu.VMEM((128, 128), F32),
            pltpu.VMEM((128, 128), I32),
            pltpu.VMEM((128, 128), I32),
            pltpu.VMEM((NALPHA * ROWS, COLS), F32),
            pltpu.VMEM((LOW, 1024), BF16),
            pltpu.VMEM((2 * HIGH * ROWS, LOW), F32),
            pltpu.VMEM((NALPHA, ROWS, COLS), F32),
            pltpu.VMEM((NALPHA, ROWS, COLS), F32),
            pltpu.VMEM((NBETA, ROWS, COLS), F32),
            pltpu.VMEM((NBETA, ROWS, COLS), F32),
            dma((NALPHA,)), dma((NALPHA,)), dma((NBETA,)), dma((NBETA,)),
            dma((NALPHA,)), dma((NALPHA,)), dma((NBETA,)), dma((NBETA,)),
        ],
        compiler_params=pltpu.CompilerParams(
            collective_id=0, has_side_effects=True, vmem_limit_bytes=48 * 1024 * 1024),
    )(vector, integrals, *lists)


def solution(mesh):
    placed = (P("alpha", "beta"), P(), P(), P(), P(), P(), P(), P())
    return jax.shard_map(
        local, mesh=mesh, in_specs=placed, out_specs=P("alpha", "beta"), check_vma=False
    )
```

```python
import jax
import jax.numpy as jnp
from jax import lax
from jax.experimental import pallas as pl
from jax.experimental.pallas import tpu as pltpu
from jax.sharding import PartitionSpec as P

MESH = pl.DeviceIdType.MESH
F32, BF16, I32 = jnp.float32, jnp.bfloat16, jnp.int32

EXC, PAIRS = 56, 196
NALPHA, NBETA = 32, 16
ROWS, COLS = 16, 192
HIGH, LOW = 12, 256
STEPS = 12
TILES = 4 * STEPS
ENTRIES = 256 * TILES


def dot(a, b):
    return lax.dot_general(a, b, (((1,), (0,)), ((), ())), preferred_element_type=F32)


def dot_t(a, b):
    return lax.dot_general(a, b, (((1,), (1,)), ((), ())), preferred_element_type=F32)


def split(x):
    high = x.astype(BF16)
    return high, (x - high.astype(F32)).astype(BF16)


def iota(shape, dim):
    return lax.broadcasted_iota(I32, shape, dim)


def codes_of(targets, pairs, signs):
    return targets * 512 + pairs * 2 + (signs > 0).astype(I32)


def stack_halves(first, second):
    pad = jnp.zeros((64 - EXC, 128), I32)
    return jnp.concatenate([first, pad, second, pad], axis=0)


def transposed(codes):
    return jnp.transpose(codes.astype(F32)).astype(I32)


def sign_of(codes, entry):
    return jnp.where((entry & 63) < EXC, ((codes & 1) * 2 - 1).astype(F32), 0.0)


def pair_of(codes):
    return (codes >> 1) & 255


def low_of(codes):
    return (codes >> 9) & 255


def one_hot(index, width, value=1.0):
    if index.shape[1] == 1:
        where = iota((index.shape[0], width), 1)
    else:
        where = iota((width, index.shape[1]), 0)
    return jnp.where(index == where, value, 0.0).astype(BF16)


def kernel(
    v_hbm, m_hbm, at_ref, ap_ref, as_ref, bt_ref, bp_ref, bs_ref,
    out_ref,
    v_ref, m_ref, alists, blists, list_sem, mpad, mh, ml,
    ga, gz, za, zsplit,
    acol, arow, a_oh_c, a_oh_r, a_kh, a_kl, asum,
    bcol, brow, b_oh_c, b_oh_r, b_k, fetched, returned, acc,
    ra_out, ra_in, rz_out, rz_in, rz_sum, rz_far,
    sa_sem, ga_sem, sz_sem, gz_sem, sra_sem, ra_sem, srz_sem, rz_sem,
):
    a, b = lax.axis_index("alpha"), lax.axis_index("beta")

    def alpha_peer(d):
        return lax.rem(a + d, NALPHA)

    def beta_peer(d):
        return lax.rem(b + d + NBETA, NBETA)

    def alpha_copy(src, dst, send, recv, d):
        return pltpu.make_async_remote_copy(
            src_ref=src, dst_ref=dst, send_sem=send.at[d], recv_sem=recv.at[d],
            device_id=(alpha_peer(d), b), device_id_type=MESH)

    def beta_copy(src, dst, send, recv, n, d):
        return pltpu.make_async_remote_copy(
            src_ref=src, dst_ref=dst, send_sem=send.at[n], recv_sem=recv.at[n],
            device_id=(a, beta_peer(d)), device_id_type=MESH)

    barrier = pltpu.get_barrier_semaphore()
    near = (4, -4, 1, -1, 2, -2)
    for d in near:
        pl.semaphore_signal(barrier, inc=1, device_id=(a, beta_peer(d)), device_id_type=MESH)

    @pl.loop(1, NALPHA)
    def _(d):
        pl.semaphore_signal(barrier, inc=1, device_id=(alpha_peer(d), b), device_id_type=MESH)

    awin = pl.multiple_of((a // 8) * 128, 128)
    bwin = pl.multiple_of((b // 2) * 384, 128)
    copies = [
        pltpu.make_async_copy(v_hbm, v_ref, list_sem.at[6]),
        pltpu.make_async_copy(m_hbm, m_ref, list_sem.at[7]),
    ]
    for i, ref in enumerate((at_ref, ap_ref, as_ref)):
        copies.append(pltpu.make_async_copy(
            ref.at[:, pl.ds(awin, 128)], alists.at[i], list_sem.at[i]))
    for i, ref in enumerate((bt_ref, bp_ref, bs_ref)):
        copies.append(pltpu.make_async_copy(
            ref.at[:, pl.ds(bwin, 384)], blists.at[i], list_sem.at[3 + i]))
    for copy in copies:
        copy.start()
    for copy in copies:
        copy.wait()

    gz[b] = v_ref[...]
    ga[a] = v_ref[...]
    mpad[...] = jnp.zeros_like(mpad)
    mpad[0:PAIRS, 0:PAIRS] = m_ref[...]
    high, low = split(mpad[...])
    mh[...] = high
    ml[...] = low

    code = codes_of(blists[0], blists[1], blists[2])
    odd = lax.rem(b, 2) == 1
    first = jnp.where(odd, pltpu.roll(code, 192, 1)[:, :128], code[:, :128])
    second = jnp.where(odd, pltpu.roll(code, 96, 1)[:, :128], pltpu.roll(code, 288, 1)[:, :128])
    code = stack_halves(first, second)
    bcol[...] = code
    brow[...] = transposed(code)

    code = codes_of(alists[0], alists[1], alists[2])
    shift = lax.rem(a, 8) * 16
    first = pltpu.roll(code, lax.rem(128 - shift, 128), 1)
    second = pltpu.roll(code, lax.rem(248 - shift, 128), 1)
    code = stack_halves(first, second)
    acol[...] = code
    arow[...] = transposed(code)

    pl.semaphore_wait(barrier, NALPHA - 1 + len(near))

    def z_first():
        return [beta_copy(v_ref, gz.at[b], sz_sem, gz_sem, n, d) for n, d in enumerate(near)]

    def z_second():
        up, down = beta_peer(4), beta_peer(-4)
        top, bottom = pl.ds(0, 8), pl.ds(8, 8)
        return [
            beta_copy(gz.at[down, top], gz.at[down, top], sz_sem, gz_sem, 6, 4),
            beta_copy(gz.at[up, bottom], gz.at[up, bottom], sz_sem, gz_sem, 7, -4),
            beta_copy(gz.at[up], gz.at[up], sz_sem, gz_sem, 8, 1),
            beta_copy(gz.at[up], gz.at[up], sz_sem, gz_sem, 9, -1),
            beta_copy(gz.at[down], gz.at[down], sz_sem, gz_sem, 10, 1),
            beta_copy(gz.at[down], gz.at[down], sz_sem, gz_sem, 11, -1),
            beta_copy(gz.at[down], gz.at[down], sz_sem, gz_sem, 12, 2),
            beta_copy(gz.at[up], gz.at[up], sz_sem, gz_sem, 13, -2),
        ]

    def z_third():
        far = beta_peer(8)
        return [
            beta_copy(gz.at[far], gz.at[far], sz_sem, gz_sem, 14, 1),
            beta_copy(gz.at[far], gz.at[far], sz_sem, gz_sem, 15, -1),
        ]

    for copy in z_first():
        copy.start()

    @pl.loop(1, NALPHA)
    def _(d):
        alpha_copy(v_ref, ga.at[a], sa_sem, ga_sem, d).start()

    left_half = iota((1, 128), 1) < 64

    def beta_step(step):
        rows = brow[pl.ds(pl.multiple_of(step * 8, 8), 8), :]
        cols = pltpu.roll(bcol[...], lax.rem(128 - 8 * step, 128), 1)
        w_c, w_r = [], []
        for k in range(8):
            at = pl.multiple_of(step * 1024 + 128 * k, 128)
            col = cols[:, k:k + 1]
            b_oh_c[pl.ds(at, 128), :] = one_hot(low_of(col), LOW)
            w_c.append(one_hot(pair_of(col), 256, sign_of(col, iota((128, 1), 0))))
            row = rows[k:k + 1, :]
            b_oh_r[:, pl.ds(at, 128)] = one_hot(low_of(row), LOW)
            w_r.append(one_hot(pair_of(row), 256, sign_of(row, iota((1, 128), 1))))
        w_c = jnp.concatenate(w_c, 0)
        uh, ul = dot_t(w_c, mh[...]).astype(BF16), dot_t(w_c, ml[...]).astype(BF16)
        for g in range(4):
            w = jnp.concatenate([w_r[2 * g], w_r[2 * g + 1]], 1)
            kh = dot(uh[256 * g:256 * g + 256], w)
            kl = dot(ul[256 * g:256 * g + 256], w)
            for j in range(4):
                sl = slice(64 * j, 64 * j + 64), slice(128 * (j // 2), 128 * (j // 2) + 128)
                one, two = kh[sl], pltpu.roll(kl[sl], 64, 1)
                mine = left_half if j % 2 == 0 else ~left_half
                b_k[step * 4 + g, 64 * j:64 * j + 64, :] = jnp.where(mine, one, two).astype(BF16)

    same = (iota((256, 256), 0) >> 6) == (iota((256, 256), 1) >> 6)

    def alpha_prepare():
        for g in range(4):
            w_c, w_r = [], []
            for k in (2 * g, 2 * g + 1):
                col, row = acol[:, k:k + 1], arow[k:k + 1, :]
                a_oh_c[128 * k:128 * k + 128, :] = one_hot(col >> 9, NALPHA * ROWS)
                a_oh_r[:, 128 * k:128 * k + 128] = one_hot(row >> 9, NALPHA * ROWS)
                w_c.append(one_hot(pair_of(col), 256, sign_of(col, iota((128, 1), 0))))
                w_r.append(one_hot(pair_of(row), 256, sign_of(row, iota((1, 128), 1))))
            w_c, w_r = jnp.concatenate(w_c, 0), jnp.concatenate(w_r, 1)
            uh, ul = dot(w_c, mh[...]).astype(BF16), dot(w_c, ml[...]).astype(BF16)
            a_kh[g] = jnp.where(same, dot(uh, w_r), 0.0).astype(BF16)
            a_kl[g] = jnp.where(same, dot(ul, w_r), 0.0).astype(BF16)

    pl.loop(0, 4)(beta_step)
    for copy in z_first():
        copy.wait_recv()
    for copy in z_second():
        copy.start()
    pl.loop(4, 8)(beta_step)
    for copy in z_second():
        copy.wait_recv()
    for copy in z_third():
        copy.start()
    alpha_prepare()
    pl.loop(8, STEPS)(beta_step)

    @pl.loop(1, NALPHA)
    def _(d):
        alpha_copy(v_ref, ga.at[a], sa_sem, ga_sem, d).wait_recv()

    vh, vl = split(ga[...].reshape(NALPHA * ROWS, COLS))
    fh, fl = dot(a_oh_c[...], vh).astype(BF16), dot(a_oh_c[...], vl).astype(BF16)
    rh, rl = [], []
    for g in range(4):
        mine = slice(256 * g, 256 * g + 256)
        high, low = split(
            dot(a_kh[g], fh[mine]) + dot(a_kh[g], fl[mine]) + dot(a_kl[g], fh[mine]))
        rh.append(high)
        rl.append(low)
    rh, rl = jnp.concatenate(rh, 0), jnp.concatenate(rl, 0)
    asum = dot(a_oh_r[...], rh) + dot(a_oh_r[...], rl)
    ra_out[...] = asum.reshape(NALPHA, ROWS, COLS)

    @pl.loop(1, NALPHA)
    def _(d):
        alpha_copy(ra_out.at[alpha_peer(d)], ra_in.at[a], sra_sem, ra_sem, d).start()

    for copy in z_third():
        copy.wait_recv()
    for i in range(NBETA):
        za[:, COLS * i:COLS * (i + 1)] = gz[i]
    for h in range(HIGH):
        high, low = split(za[:, LOW * h:LOW * (h + 1)])
        zsplit[32 * h:32 * h + 16, :] = high
        zsplit[32 * h + 16:32 * h + 32, :] = low
    acc[...] = jnp.zeros_like(acc)

    quarter = iota((1, 256), 1) >> 6

    def high_rows(step):
        return brow[pl.ds(pl.multiple_of(step * 8, 8), 8), :] >> 17

    def pair_row(rows, g):
        return jnp.concatenate([rows[2 * g:2 * g + 1, :], rows[2 * g + 1:2 * g + 2, :]], axis=1)

    @pl.loop(0, STEPS)
    def _(step):
        highs = high_rows(step)
        for g in range(4):
            at = pl.multiple_of(step * 1024 + 256 * g, 256)
            picked = dot(zsplit[...], b_oh_r[:, pl.ds(at, 256)])
            hrow = pair_row(highs, g)
            f = picked[0:32]
            for h in range(1, HIGH):
                f = jnp.where(hrow == h, picked[32 * h:32 * h + 32], f)
            fetched[:, pl.ds(at, 256)] = f.astype(BF16)

    @pl.loop(0, STEPS)
    def _(step):
        for g in range(4):
            at = pl.multiple_of(step * 1024 + 256 * g, 256)
            f = fetched[:, pl.ds(at, 256)].astype(F32)
            lhs = jnp.concatenate(
                [jnp.where(quarter == j, f, 0.0).astype(BF16) for j in range(4)], axis=0)
            back = dot(lhs, b_k[step * 4 + g])
            parts = []
            for j in (0, 2):
                h0, l0 = back[32 * j:32 * j + 16], back[32 * j + 16:32 * j + 32]
                h1, l1 = back[32 * j + 32:32 * j + 48], back[32 * j + 48:32 * j + 64]
                parts.append(jnp.where(left_half, h0 + l0, h1 + l1)
                             + pltpu.roll(jnp.where(left_half, h1, h0), 64, 1))
            r = jnp.concatenate(parts, 1)
            high, low = split(r)
            returned[0:16, pl.ds(at, 256)] = high
            returned[16:32, pl.ds(at, 256)] = low

    @pl.loop(0, STEPS)
    def _(step):
        highs = high_rows(step)
        lhs = []
        for g in range(4):
            at = pl.multiple_of(step * 1024 + 256 * g, 256)
            r = returned[:, pl.ds(at, 256)].astype(F32)
            hrow = pair_row(highs, g)
            lhs.append(jnp.concatenate(
                [jnp.where(hrow == h, r, 0.0).astype(BF16) for h in range(HIGH)], axis=0))
        at = pl.multiple_of(step * 1024, 1024)
        acc[...] += dot(jnp.concatenate(lhs, 1), b_oh_c[pl.ds(at, 1024), :])

    for h in range(HIGH):
        za[:, LOW * h:LOW * (h + 1)] = acc[32 * h:32 * h + 16, :] + acc[32 * h + 16:32 * h + 32, :]
    for i in range(NBETA):
        rz_out[i] = za[:, COLS * i:COLS * (i + 1)]

    def near_copies():
        made = []
        for n, (d, k) in enumerate(((1, 2), (-1, 2), (1, 1), (-1, 1), (1, 3), (-1, 3), (2, 1),
                                    (-2, 3), (1, 0), (-1, 0), (2, 0), (-2, 0))):
            made.append(beta_copy(rz_out.at[beta_peer(d + 4 * k)], rz_in.at[n], srz_sem, rz_sem, n, d))
        return made

    made = near_copies()
    for copy in made:
        copy.start()
    top, bottom = pl.ds(0, 8), pl.ds(8, 8)
    far = [
        beta_copy(rz_sum.at[2, top], rz_far.at[0, top], srz_sem, rz_sem, 12, 4),
        beta_copy(rz_sum.at[2, bottom], rz_far.at[0, bottom], srz_sem, rz_sem, 13, -4),
        beta_copy(rz_sum.at[1], rz_far.at[1], srz_sem, rz_sem, 14, 4),
        beta_copy(rz_sum.at[3], rz_far.at[2], srz_sem, rz_sem, 15, -4),
    ]
    made[0].wait_recv()
    made[1].wait_recv()
    rz_sum[2] = rz_out[beta_peer(8)] + rz_in[0] + rz_in[1]
    far[0].start()
    far[1].start()
    for n in range(2, 12):
        made[n].wait_recv()
    s1 = rz_out[beta_peer(4)] + rz_in[2] + rz_in[3] + rz_in[6]
    s3 = rz_out[beta_peer(12)] + rz_in[4] + rz_in[5] + rz_in[7]
    total = rz_out[b] + rz_in[8] + rz_in[9] + rz_in[10] + rz_in[11]
    far[0].wait_recv()
    far[1].wait_recv()
    rz_sum[1, 0:8] = s1[0:8] + rz_far[0, 0:8]
    rz_sum[1, 8:16] = s1[8:16]
    rz_sum[3, 0:8] = s3[0:8]
    rz_sum[3, 8:16] = s3[8:16] + rz_far[0, 8:16]
    far[2].start()
    far[3].start()

    total = total + ra_out[a]

    @pl.loop(1, NALPHA)
    def _(d):
        alpha_copy(v_ref, ga.at[a], sa_sem, ga_sem, d).wait_send()
        alpha_copy(ra_out.at[alpha_peer(d)], ra_in.at[a], sra_sem, ra_sem, d).wait()

    ra_in[a] = jnp.zeros((ROWS, COLS), F32)
    for i in range(NALPHA):
        total = total + ra_in[i]
    for copy in z_first() + z_second() + z_third() + made + far:
        copy.wait_send()
    far[2].wait_recv()
    far[3].wait_recv()
    out_ref[...] = total + rz_far[1] + rz_far[2]


def local(vector, integrals, *lists):
    vmem = pl.BlockSpec(memory_space=pltpu.VMEM)
    hbm = pl.BlockSpec(memory_space=pltpu.HBM)
    dma = pltpu.SemaphoreType.DMA

    def block(*shape):
        return pltpu.VMEM(shape, F32)

    return pl.pallas_call(
        kernel,
        out_shape=jax.ShapeDtypeStruct((ROWS, COLS), F32),
        in_specs=[hbm] * 8,
        out_specs=vmem,
        scratch_shapes=[
            block(ROWS, COLS),
            block(PAIRS, PAIRS),
            pltpu.VMEM((3, EXC, 128), I32),
            pltpu.VMEM((3, EXC, 384), I32),
            dma((8,)),
            block(256, 256),
            pltpu.VMEM((256, 256), BF16),
            pltpu.VMEM((256, 256), BF16),
            block(NALPHA, ROWS, COLS),
            block(NBETA, ROWS, COLS),
            block(ROWS, NBETA * COLS),
            pltpu.VMEM((2 * HIGH * ROWS, LOW), BF16),
            pltpu.VMEM((128, 128), I32),
            pltpu.VMEM((128, 128), I32),
            pltpu.VMEM((1024, NALPHA * ROWS), BF16),
            pltpu.VMEM((NALPHA * ROWS, 1024), BF16),
            pltpu.VMEM((4, 256, 256), BF16),
            pltpu.VMEM((4, 256, 256), BF16),
            block(NALPHA * ROWS, COLS),
            pltpu.VMEM((128, 128), I32),
            pltpu.VMEM((128, 128), I32),
            pltpu.VMEM((ENTRIES, LOW), BF16),
            pltpu.VMEM((LOW, ENTRIES), BF16),
            pltpu.VMEM((TILES, 256, 128), BF16),
            pltpu.VMEM((2 * ROWS, ENTRIES), BF16),
            pltpu.VMEM((2 * ROWS, ENTRIES), BF16),
            block(2 * HIGH * ROWS, LOW),
            block(NALPHA, ROWS, COLS),
            block(NALPHA, ROWS, COLS),
            block(NBETA, ROWS, COLS),
            block(12, ROWS, COLS),
            block(4, ROWS, COLS),
            block(3, ROWS, COLS),
            dma((NALPHA,)), dma((NALPHA,)), dma((NBETA,)), dma((NBETA,)),
            dma((NALPHA,)), dma((NALPHA,)), dma((NBETA,)), dma((NBETA,)),
        ],
        compiler_params=pltpu.CompilerParams(
            collective_id=0, has_side_effects=True, vmem_limit_bytes=52 * 1024 * 1024),
    )(vector, integrals, *lists)


def solution(mesh):
    placed = (P("alpha", "beta"), P(), P(), P(), P(), P(), P(), P())
    return jax.shard_map(
        local, mesh=mesh, in_specs=placed, out_specs=P("alpha", "beta"), check_vma=False
    )
```

```python
import jax
import jax.numpy as jnp
from jax import lax
from jax.experimental import pallas as pl
from jax.experimental.pallas import tpu as pltpu
from jax.sharding import PartitionSpec as P

MESH = pl.DeviceIdType.MESH
F32, BF16, I32 = jnp.float32, jnp.bfloat16, jnp.int32

EXC, PAIRS = 56, 196
NALPHA, NBETA = 32, 16
ROWS, COLS = 16, 192
HIGH, LOW = 12, 256
STEPS = 12
TILES = 4 * STEPS
ENTRIES = 256 * TILES


def dot(a, b):
    return lax.dot_general(a, b, (((1,), (0,)), ((), ())), preferred_element_type=F32)


def dot_t(a, b):
    return lax.dot_general(a, b, (((1,), (1,)), ((), ())), preferred_element_type=F32)


def split(x):
    high = x.astype(BF16)
    return high, (x - high.astype(F32)).astype(BF16)


def iota(shape, dim):
    return lax.broadcasted_iota(I32, shape, dim)


def codes_of(targets, pairs, signs):
    return targets * 512 + pairs * 2 + (signs > 0).astype(I32)


def stack_halves(first, second):
    pad = jnp.zeros((64 - EXC, 128), I32)
    return jnp.concatenate([first, pad, second, pad], axis=0)


def transposed(codes):
    return jnp.transpose(codes.astype(F32)).astype(I32)


def sign_of(codes, entry):
    return jnp.where((entry & 63) < EXC, ((codes & 1) * 2 - 1).astype(F32), 0.0)


def pair_of(codes):
    return (codes >> 1) & 255


def low_of(codes):
    return (codes >> 9) & 255


def to_bf16(x):
    return x.astype(F32).astype(BF16)


def row_hot(index, width, value=None):
    n = index.shape[1]
    value = jnp.ones((16, n), BF16) if value is None else to_bf16(jnp.broadcast_to(value, (16, n)))
    here = to_bf16(iota((16, n), 0))
    out = []
    for start in range(0, width, 256):
        near = to_bf16(jnp.broadcast_to(index - start, (16, n)))
        out += [jnp.where(here == near - jnp.asarray(s, BF16), value, jnp.zeros((16, n), BF16))
                for s in range(0, min(256, width - start), 16)]
    return jnp.concatenate(out, 0)


def col_hot(index, width, value=None):
    n = index.shape[0]
    value = jnp.ones((n, 128), BF16) if value is None else to_bf16(jnp.broadcast_to(value, (n, 128)))
    here = to_bf16(iota((n, 128), 1))
    out = []
    for start in range(0, width, 256):
        near = to_bf16(jnp.broadcast_to(index - start, (n, 128)))
        out += [jnp.where(here == near - jnp.asarray(s, BF16), value, jnp.zeros((n, 128), BF16))
                for s in range(0, min(256, width - start), 128)]
    return jnp.concatenate(out, 1)


def swap(x):
    return pltpu.roll(x, 64, x.ndim - 1)


def pack_tail(tail):
    return jnp.where(iota((1, 128), 1) < 64, tail[..., 0:8, :], swap(tail[..., 8:16, :]))


def unpack_tail(packed):
    return jnp.concatenate([packed, swap(packed)], axis=-2)


def kernel(
    v_hbm, m_hbm, at_ref, ap_ref, as_ref, bt_ref, bp_ref, bs_ref,
    out_ref,
    v_ref, wide, vp, m_ref, alists, blists, list_sem, mpad, mh, ml,
    ga, gz, za, zsplit,
    acol, arow, a_oh_c, a_oh_r, a_kh, a_kl,
    bcol, brow, b_oh_c, b_oh_r, b_k, fetched, returned, acc,
    ra_out, ra_in, rz_out, rz_in,
    sa_sem, ga_sem, sz_sem, gz_sem, sra_sem, ra_sem, srz_sem, rz_sem,
):
    a, b = lax.axis_index("alpha"), lax.axis_index("beta")

    def alpha_peer(d):
        return lax.rem(a + d, NALPHA)

    def beta_peer(d):
        return lax.rem(b + d, NBETA)

    def alpha_copy(src, dst, send, recv, d):
        return pltpu.make_async_remote_copy(
            src_ref=src, dst_ref=dst, send_sem=send.at[d], recv_sem=recv.at[d],
            device_id=(alpha_peer(d), b), device_id_type=MESH)

    def beta_copy(src, dst, send, recv, d):
        return pltpu.make_async_remote_copy(
            src_ref=src, dst_ref=dst, send_sem=send.at[d], recv_sem=recv.at[d],
            device_id=(a, beta_peer(d)), device_id_type=MESH)

    barrier = pltpu.get_barrier_semaphore()

    @pl.loop(1, NBETA)
    def _(d):
        pl.semaphore_signal(barrier, inc=1, device_id=(a, beta_peer(d)), device_id_type=MESH)

    @pl.loop(1, NALPHA)
    def _(d):
        pl.semaphore_signal(barrier, inc=1, device_id=(alpha_peer(d), b), device_id_type=MESH)

    awin = pl.multiple_of((a // 8) * 128, 128)
    bwin = pl.multiple_of((b // 2) * 384, 128)
    copies = [
        pltpu.make_async_copy(v_hbm, v_ref, list_sem.at[6]),
        pltpu.make_async_copy(m_hbm, m_ref, list_sem.at[7]),
    ]
    for i, ref in enumerate((at_ref, ap_ref, as_ref)):
        copies.append(pltpu.make_async_copy(
            ref.at[:, pl.ds(awin, 128)], alists.at[i], list_sem.at[i]))
    for i, ref in enumerate((bt_ref, bp_ref, bs_ref)):
        copies.append(pltpu.make_async_copy(
            ref.at[:, pl.ds(bwin, 384)], blists.at[i], list_sem.at[3 + i]))
    for copy in copies:
        copy.start()
    for copy in copies:
        copy.wait()

    left_half = iota((1, 128), 1) < 64
    wide[:, 0:COLS] = v_ref[...]
    vp[0:16, :] = wide[:, 0:128]
    vp[16:24, :] = pack_tail(wide[:, 128:256])
    gz[b] = vp[...]
    ga[a] = vp[...]
    mpad[...] = jnp.zeros_like(mpad)
    mpad[0:PAIRS, 0:PAIRS] = m_ref[...]
    high, low = split(mpad[...])
    mh[...] = high
    ml[...] = low

    code = codes_of(blists[0], blists[1], blists[2])
    odd = lax.rem(b, 2) == 1
    first = jnp.where(odd, pltpu.roll(code, 192, 1)[:, :128], code[:, :128])
    second = jnp.where(odd, pltpu.roll(code, 96, 1)[:, :128], pltpu.roll(code, 288, 1)[:, :128])
    code = stack_halves(first, second)
    bcol[...] = code
    brow[...] = transposed(code)

    code = codes_of(alists[0], alists[1], alists[2])
    shift = lax.rem(a, 8) * 16
    first = pltpu.roll(code, lax.rem(128 - shift, 128), 1)
    second = pltpu.roll(code, lax.rem(248 - shift, 128), 1)
    code = stack_halves(first, second)
    acol[...] = code
    arow[...] = transposed(code)

    def beta_step(step):
        rows = brow[pl.ds(pl.multiple_of(step * 8, 8), 8), :]
        cols = pltpu.roll(bcol[...], lax.rem(128 - 8 * step, 128), 1)
        w_c, w_r = [], []
        for k in range(8):
            at = pl.multiple_of(step * 1024 + 128 * k, 128)
            col = cols[:, k:k + 1]
            b_oh_c[pl.ds(at, 128), :] = col_hot(low_of(col), LOW)
            w_c.append(col_hot(pair_of(col), 256, sign_of(col, iota((128, 1), 0))))
            row = rows[k:k + 1, :]
            b_oh_r[:, pl.ds(at, 128)] = row_hot(low_of(row), LOW)
            w_r.append(row_hot(pair_of(row), 256, sign_of(row, iota((1, 128), 1))))
        w_c = jnp.concatenate(w_c, 0)
        uh, ul = dot_t(w_c, mh[...]).astype(BF16), dot_t(w_c, ml[...]).astype(BF16)
        for g in range(4):
            w = jnp.concatenate([w_r[2 * g], w_r[2 * g + 1]], 1)
            kh = dot(uh[256 * g:256 * g + 256], w)
            kl = dot(ul[256 * g:256 * g + 256], w)
            for j in range(4):
                sl = slice(64 * j, 64 * j + 64), slice(128 * (j // 2), 128 * (j // 2) + 128)
                one, two = kh[sl], pltpu.roll(kl[sl], 64, 1)
                mine = left_half if j % 2 == 0 else ~left_half
                b_k[step * 4 + g, 64 * j:64 * j + 64, :] = jnp.where(mine, one, two).astype(BF16)

    same = (iota((256, 256), 0) >> 6) == (iota((256, 256), 1) >> 6)

    def alpha_prepare():
        for g in range(4):
            w_c, w_r = [], []
            for k in (2 * g, 2 * g + 1):
                col, row = acol[:, k:k + 1], arow[k:k + 1, :]
                a_oh_c[128 * k:128 * k + 128, :] = col_hot(col >> 9, NALPHA * ROWS)
                a_oh_r[:, 128 * k:128 * k + 128] = row_hot(row >> 9, NALPHA * ROWS)
                w_c.append(col_hot(pair_of(col), 256, sign_of(col, iota((128, 1), 0))))
                w_r.append(row_hot(pair_of(row), 256, sign_of(row, iota((1, 128), 1))))
            w_c, w_r = jnp.concatenate(w_c, 0), jnp.concatenate(w_r, 1)
            uh, ul = dot(w_c, mh[...]).astype(BF16), dot(w_c, ml[...]).astype(BF16)
            a_kh[g] = jnp.where(same, dot(uh, w_r), 0.0).astype(BF16)
            a_kl[g] = jnp.where(same, dot(ul, w_r), 0.0).astype(BF16)

    pl.loop(0, 4, unroll=4)(beta_step)
    pl.semaphore_wait(barrier, NALPHA + NBETA - 2)

    @pl.loop(1, NBETA)
    def _(d):
        beta_copy(vp, gz.at[b], sz_sem, gz_sem, d).start()

    @pl.loop(1, NALPHA)
    def _(d):
        alpha_copy(vp, ga.at[a], sa_sem, ga_sem, d).start()

    alpha_prepare()
    pl.loop(4, STEPS, unroll=4)(beta_step)

    @pl.loop(1, NALPHA)
    def _(d):
        alpha_copy(vp, ga.at[a], sa_sem, ga_sem, d).wait_recv()

    vh, vl = split(jnp.concatenate(
        [ga[:, 0:16, :].reshape(512, 128), unpack_tail(ga[:, 16:24, :]).reshape(512, 128)], axis=1))
    fh, fl = dot(a_oh_c[...], vh).astype(BF16), dot(a_oh_c[...], vl).astype(BF16)
    rh, rl = [], []
    for g in range(4):
        mine = slice(256 * g, 256 * g + 256)
        high, low = split(
            dot(a_kh[g], fh[mine]) + dot(a_kh[g], fl[mine]) + dot(a_kl[g], fh[mine]))
        rh.append(high)
        rl.append(low)
    rh, rl = jnp.concatenate(rh, 0), jnp.concatenate(rl, 0)
    asum = dot(a_oh_r[...], rh) + dot(a_oh_r[...], rl)
    ra_out[:, 0:16, :] = asum[:, 0:128].reshape(NALPHA, 16, 128)
    ra_out[:, 16:24, :] = pack_tail(asum[:, 128:256].reshape(NALPHA, 16, 128))

    @pl.loop(1, NALPHA)
    def _(d):
        alpha_copy(ra_out.at[alpha_peer(d)], ra_in.at[a], sra_sem, ra_sem, d).start()

    @pl.loop(1, NBETA)
    def _(d):
        beta_copy(vp, gz.at[b], sz_sem, gz_sem, d).wait_recv()

    for m in range(NBETA // 2):
        first, second = gz[2 * m], gz[2 * m + 1]
        turned = swap(second[0:16])
        za[:, 384 * m:384 * m + 128] = first[0:16]
        za[:, 384 * m + 128:384 * m + 256] = jnp.where(left_half, unpack_tail(first[16:24]), turned)
        za[:, 384 * m + 256:384 * m + 384] = jnp.where(
            left_half, turned, swap(unpack_tail(second[16:24])))
    for h in range(HIGH):
        high, low = split(za[:, LOW * h:LOW * (h + 1)])
        zsplit[32 * h:32 * h + 16, :] = high
        zsplit[32 * h + 16:32 * h + 32, :] = low
    acc[...] = jnp.zeros_like(acc)

    quarter = iota((1, 256), 1) >> 6

    def high_rows(step):
        return brow[pl.ds(pl.multiple_of(step * 8, 8), 8), :] >> 17

    def pair_row(rows, g):
        return jnp.concatenate([rows[2 * g:2 * g + 1, :], rows[2 * g + 1:2 * g + 2, :]], axis=1)

    @pl.loop(0, STEPS, unroll=3)
    def _(step):
        highs = high_rows(step)
        for g in range(4):
            at = pl.multiple_of(step * 1024 + 256 * g, 256)
            picked = dot(zsplit[...], b_oh_r[:, pl.ds(at, 256)])
            hrow = pair_row(highs, g)
            f = picked[0:32]
            for h in range(1, HIGH):
                f = jnp.where(hrow == h, picked[32 * h:32 * h + 32], f)
            fetched[:, pl.ds(at, 256)] = f.astype(BF16)

    @pl.loop(0, STEPS, unroll=3)
    def _(step):
        for g in range(4):
            at = pl.multiple_of(step * 1024 + 256 * g, 256)
            f = fetched[:, pl.ds(at, 256)].astype(F32)
            lhs = jnp.concatenate(
                [jnp.where(quarter == j, f, 0.0).astype(BF16) for j in range(4)], axis=0)
            back = dot(lhs, b_k[step * 4 + g])
            parts = []
            for j in (0, 2):
                h0, l0 = back[32 * j:32 * j + 16], back[32 * j + 16:32 * j + 32]
                h1, l1 = back[32 * j + 32:32 * j + 48], back[32 * j + 48:32 * j + 64]
                parts.append(jnp.where(left_half, h0 + l0, h1 + l1)
                             + pltpu.roll(jnp.where(left_half, h1, h0), 64, 1))
            r = jnp.concatenate(parts, 1)
            high, low = split(r)
            returned[0:16, pl.ds(at, 256)] = high
            returned[16:32, pl.ds(at, 256)] = low

    @pl.loop(0, STEPS, unroll=3)
    def _(step):
        highs = high_rows(step)
        lhs = []
        for g in range(4):
            at = pl.multiple_of(step * 1024 + 256 * g, 256)
            r = returned[:, pl.ds(at, 256)].astype(F32)
            hrow = pair_row(highs, g)
            lhs.append(jnp.concatenate(
                [jnp.where(hrow == h, r, 0.0).astype(BF16) for h in range(HIGH)], axis=0))
        at = pl.multiple_of(step * 1024, 1024)
        acc[...] += dot(jnp.concatenate(lhs, 1), b_oh_c[pl.ds(at, 1024), :])

    for h in range(HIGH):
        za[:, LOW * h:LOW * (h + 1)] = acc[32 * h:32 * h + 16, :] + acc[32 * h + 16:32 * h + 32, :]
    for m in range(NBETA // 2):
        t0 = za[:, 384 * m:384 * m + 128]
        t1 = za[:, 384 * m + 128:384 * m + 256]
        t2 = za[:, 384 * m + 256:384 * m + 384]
        rz_out[2 * m, 0:16] = t0
        rz_out[2 * m, 16:24] = pack_tail(t1)
        rz_out[2 * m + 1, 0:16] = swap(jnp.where(left_half, t2, t1))
        rz_out[2 * m + 1, 16:24] = pack_tail(swap(t2))

    @pl.loop(1, NBETA)
    def _(d):
        beta_copy(rz_out.at[beta_peer(d)], rz_in.at[b], srz_sem, rz_sem, d).start()

    ra_in[a] = ra_out[a]
    rz_in[b] = rz_out[b]

    @pl.loop(1, NALPHA)
    def _(d):
        alpha_copy(vp, ga.at[a], sa_sem, ga_sem, d).wait_send()
        alpha_copy(ra_out.at[alpha_peer(d)], ra_in.at[a], sra_sem, ra_sem, d).wait()

    total = ra_in[0]
    for i in range(1, NALPHA):
        total = total + ra_in[i]

    @pl.loop(1, NBETA)
    def _(d):
        beta_copy(vp, gz.at[b], sz_sem, gz_sem, d).wait_send()
        beta_copy(rz_out.at[beta_peer(d)], rz_in.at[b], srz_sem, rz_sem, d).wait()

    for i in range(NBETA):
        total = total + rz_in[i]
    out_ref[:, 0:128] = total[0:16]
    out_ref[:, 128:COLS] = unpack_tail(total[16:24])[:, 0:COLS - 128]


def local(vector, integrals, *lists):
    vmem = pl.BlockSpec(memory_space=pltpu.VMEM)
    hbm = pl.BlockSpec(memory_space=pltpu.HBM)
    dma = pltpu.SemaphoreType.DMA

    def block(*shape):
        return pltpu.VMEM(shape, F32)

    return pl.pallas_call(
        kernel,
        out_shape=jax.ShapeDtypeStruct((ROWS, COLS), F32),
        in_specs=[hbm] * 8,
        out_specs=vmem,
        scratch_shapes=[
            block(ROWS, COLS),
            block(ROWS, 256),
            block(24, 128),
            block(PAIRS, PAIRS),
            pltpu.VMEM((3, EXC, 128), I32),
            pltpu.VMEM((3, EXC, 384), I32),
            dma((8,)),
            block(256, 256),
            pltpu.VMEM((256, 256), BF16),
            pltpu.VMEM((256, 256), BF16),
            block(NALPHA, 24, 128),
            block(NBETA, 24, 128),
            block(ROWS, NBETA * COLS),
            pltpu.VMEM((2 * HIGH * ROWS, LOW), BF16),
            pltpu.VMEM((128, 128), I32),
            pltpu.VMEM((128, 128), I32),
            pltpu.VMEM((1024, NALPHA * ROWS), BF16),
            pltpu.VMEM((NALPHA * ROWS, 1024), BF16),
            pltpu.VMEM((4, 256, 256), BF16),
            pltpu.VMEM((4, 256, 256), BF16),
            pltpu.VMEM((128, 128), I32),
            pltpu.VMEM((128, 128), I32),
            pltpu.VMEM((ENTRIES, LOW), BF16),
            pltpu.VMEM((LOW, ENTRIES), BF16),
            pltpu.VMEM((TILES, 256, 128), BF16),
            pltpu.VMEM((2 * ROWS, ENTRIES), BF16),
            pltpu.VMEM((2 * ROWS, ENTRIES), BF16),
            block(2 * HIGH * ROWS, LOW),
            block(NALPHA, 24, 128),
            block(NALPHA, 24, 128),
            block(NBETA, 24, 128),
            block(NBETA, 24, 128),
            dma((NALPHA,)), dma((NALPHA,)), dma((NBETA,)), dma((NBETA,)),
            dma((NALPHA,)), dma((NALPHA,)), dma((NBETA,)), dma((NBETA,)),
        ],
        compiler_params=pltpu.CompilerParams(
            collective_id=0, has_side_effects=True, vmem_limit_bytes=54 * 1024 * 1024),
    )(vector, integrals, *lists)


def solution(mesh):
    placed = (P("alpha", "beta"), P(), P(), P(), P(), P(), P(), P())
    return jax.shard_map(
        local, mesh=mesh, in_specs=placed, out_specs=P("alpha", "beta"), check_vma=False
    )
```

```python
import jax
import jax.numpy as jnp
from jax import lax
from jax.experimental import pallas as pl
from jax.experimental.pallas import tpu as pltpu
from jax.sharding import PartitionSpec as P

MESH = pl.DeviceIdType.MESH
F32, BF16, I32 = jnp.float32, jnp.bfloat16, jnp.int32

EXC, PAIRS = 56, 196
NALPHA, NBETA = 32, 16
ROWS, COLS = 16, 192
HIGH, LOW = 12, 256
STEPS = 12
TILES = 4 * STEPS
ENTRIES = 256 * TILES


def dot(a, b):
    return lax.dot_general(a, b, (((1,), (0,)), ((), ())), preferred_element_type=F32)


def dot_t(a, b):
    return lax.dot_general(a, b, (((1,), (1,)), ((), ())), preferred_element_type=F32)


def split(x):
    high = x.astype(BF16)
    return high, (x - high.astype(F32)).astype(BF16)


def iota(shape, dim):
    return lax.broadcasted_iota(I32, shape, dim)


def codes_of(targets, pairs, signs):
    return targets * 512 + pairs * 2 + (signs > 0).astype(I32)


def stack_halves(first, second):
    pad = jnp.zeros((64 - EXC, 128), I32)
    return jnp.concatenate([first, pad, second, pad], axis=0)


def transposed(codes):
    return jnp.transpose(codes.astype(F32)).astype(I32)


def sign_of(codes, entry):
    return jnp.where((entry & 63) < EXC, ((codes & 1) * 2 - 1).astype(F32), 0.0)


def pair_of(codes):
    return (codes >> 1) & 255


def low_of(codes):
    return (codes >> 9) & 255


def to_bf16(x):
    return x.astype(F32).astype(BF16)


def row_hot(index, width, value=None):
    n = index.shape[1]
    value = jnp.ones((16, n), BF16) if value is None else to_bf16(jnp.broadcast_to(value, (16, n)))
    here = to_bf16(iota((16, n), 0))
    out = []
    for start in range(0, width, 256):
        near = to_bf16(jnp.broadcast_to(index - start, (16, n)))
        out += [jnp.where(here == near - jnp.asarray(s, BF16), value, jnp.zeros((16, n), BF16))
                for s in range(0, min(256, width - start), 16)]
    return jnp.concatenate(out, 0)


def col_hot(index, width, value=None):
    n = index.shape[0]
    value = jnp.ones((n, 128), BF16) if value is None else to_bf16(jnp.broadcast_to(value, (n, 128)))
    here = to_bf16(iota((n, 128), 1))
    out = []
    for start in range(0, width, 256):
        near = to_bf16(jnp.broadcast_to(index - start, (n, 128)))
        out += [jnp.where(here == near - jnp.asarray(s, BF16), value, jnp.zeros((n, 128), BF16))
                for s in range(0, min(256, width - start), 128)]
    return jnp.concatenate(out, 1)


def swap(x):
    return pltpu.roll(x, 64, x.ndim - 1)


def pack_tail(tail):
    return jnp.where(iota((1, 128), 1) < 64, tail[..., 0:8, :], swap(tail[..., 8:16, :]))


def unpack_tail(packed):
    return jnp.concatenate([packed, swap(packed)], axis=-2)


def kernel(
    v_hbm, m_hbm, at_ref, ap_ref, as_ref, bt_ref, bp_ref, bs_ref,
    out_ref,
    v_ref, wide, vp, m_ref, alists, blists, list_sem, mpad, mh, ml,
    ga, gz, za, zsplit,
    acol, arow, a_oh_c, a_oh_r, a_kh, a_kl,
    bcol, brow, b_oh_c, b_oh_r, b_k, fetched, returned, acc,
    ra_out, ra_in, rz_out, rz_in,
    sa_sem, ga_sem, sz_sem, gz_sem, sra_sem, ra_sem, srz_sem, rz_sem,
):
    a, b = lax.axis_index("alpha"), lax.axis_index("beta")

    def alpha_peer(d):
        return lax.rem(a + d, NALPHA)

    def beta_peer(d):
        return lax.rem(b + d, NBETA)

    def alpha_copy(src, dst, send, recv, d):
        return pltpu.make_async_remote_copy(
            src_ref=src, dst_ref=dst, send_sem=send.at[d], recv_sem=recv.at[d],
            device_id=(alpha_peer(d), b), device_id_type=MESH)

    def beta_copy(src, dst, send, recv, d):
        return pltpu.make_async_remote_copy(
            src_ref=src, dst_ref=dst, send_sem=send.at[d], recv_sem=recv.at[d],
            device_id=(a, beta_peer(d)), device_id_type=MESH)

    barrier = pltpu.get_barrier_semaphore()

    @pl.loop(1, NBETA)
    def _(d):
        pl.semaphore_signal(barrier, inc=1, device_id=(a, beta_peer(d)), device_id_type=MESH)

    @pl.loop(1, NALPHA)
    def _(d):
        pl.semaphore_signal(barrier, inc=1, device_id=(alpha_peer(d), b), device_id_type=MESH)

    awin = pl.multiple_of((a // 8) * 128, 128)
    bwin = pl.multiple_of((b // 2) * 384, 128)
    copies = [
        pltpu.make_async_copy(v_hbm, v_ref, list_sem.at[6]),
        pltpu.make_async_copy(m_hbm, m_ref, list_sem.at[7]),
    ]
    for i, ref in enumerate((at_ref, ap_ref, as_ref)):
        copies.append(pltpu.make_async_copy(
            ref.at[:, pl.ds(awin, 128)], alists.at[i], list_sem.at[i]))
    for i, ref in enumerate((bt_ref, bp_ref, bs_ref)):
        copies.append(pltpu.make_async_copy(
            ref.at[:, pl.ds(bwin, 384)], blists.at[i], list_sem.at[3 + i]))
    for copy in copies:
        copy.start()
    for copy in copies:
        copy.wait()

    left_half = iota((1, 128), 1) < 64
    wide[:, 0:COLS] = v_ref[...]
    vp[0:16, :] = wide[:, 0:128]
    vp[16:24, :] = pack_tail(wide[:, 128:256])
    gz[b] = vp[...]
    ga[a] = vp[...]
    mpad[...] = jnp.zeros_like(mpad)
    mpad[0:PAIRS, 0:PAIRS] = m_ref[...]
    high, low = split(mpad[...])
    mh[...] = high
    ml[...] = low

    code = codes_of(blists[0], blists[1], blists[2])
    odd = lax.rem(b, 2) == 1
    first = jnp.where(odd, pltpu.roll(code, 192, 1)[:, :128], code[:, :128])
    second = jnp.where(odd, pltpu.roll(code, 96, 1)[:, :128], pltpu.roll(code, 288, 1)[:, :128])
    code = stack_halves(first, second)
    bcol[...] = code
    brow[...] = transposed(code)

    code = codes_of(alists[0], alists[1], alists[2])
    shift = lax.rem(a, 8) * 16
    first = pltpu.roll(code, lax.rem(128 - shift, 128), 1)
    second = pltpu.roll(code, lax.rem(248 - shift, 128), 1)
    code = stack_halves(first, second)
    acol[...] = code
    arow[...] = transposed(code)

    def beta_step(step):
        rows = brow[pl.ds(pl.multiple_of(step * 8, 8), 8), :]
        cols = pltpu.roll(bcol[...], lax.rem(128 - 8 * step, 128), 1)
        w_c, w_r = [], []
        for k in range(8):
            at = pl.multiple_of(step * 1024 + 128 * k, 128)
            col = cols[:, k:k + 1]
            b_oh_c[pl.ds(at, 128), :] = col_hot(low_of(col), LOW)
            w_c.append(col_hot(pair_of(col), 256, sign_of(col, iota((128, 1), 0))))
            row = rows[k:k + 1, :]
            b_oh_r[:, pl.ds(at, 128)] = row_hot(low_of(row), LOW)
            w_r.append(row_hot(pair_of(row), 256, sign_of(row, iota((1, 128), 1))))
        w_c = jnp.concatenate(w_c, 0)
        uh, ul = dot_t(w_c, mh[...]).astype(BF16), dot_t(w_c, ml[...]).astype(BF16)
        for g in range(4):
            w = jnp.concatenate([w_r[2 * g], w_r[2 * g + 1]], 1)
            kh = dot(uh[256 * g:256 * g + 256], w)
            kl = dot(ul[256 * g:256 * g + 256], w)
            for j in range(4):
                sl = slice(64 * j, 64 * j + 64), slice(128 * (j // 2), 128 * (j // 2) + 128)
                one, two = kh[sl], pltpu.roll(kl[sl], 64, 1)
                mine = left_half if j % 2 == 0 else ~left_half
                b_k[step * 4 + g, 64 * j:64 * j + 64, :] = jnp.where(mine, one, two).astype(BF16)

    same = (iota((256, 256), 0) >> 6) == (iota((256, 256), 1) >> 6)

    def alpha_prepare():
        for g in range(4):
            w_c, w_r = [], []
            for k in (2 * g, 2 * g + 1):
                col, row = acol[:, k:k + 1], arow[k:k + 1, :]
                a_oh_c[128 * k:128 * k + 128, :] = col_hot(col >> 9, NALPHA * ROWS)
                a_oh_r[:, 128 * k:128 * k + 128] = row_hot(row >> 9, NALPHA * ROWS)
                w_c.append(col_hot(pair_of(col), 256, sign_of(col, iota((128, 1), 0))))
                w_r.append(row_hot(pair_of(row), 256, sign_of(row, iota((1, 128), 1))))
            w_c, w_r = jnp.concatenate(w_c, 0), jnp.concatenate(w_r, 1)
            uh, ul = dot(w_c, mh[...]).astype(BF16), dot(w_c, ml[...]).astype(BF16)
            a_kh[g] = jnp.where(same, dot(uh, w_r), 0.0).astype(BF16)
            a_kl[g] = jnp.where(same, dot(ul, w_r), 0.0).astype(BF16)

    pl.loop(0, 4, unroll=4)(beta_step)
    pl.semaphore_wait(barrier, NALPHA + NBETA - 2)

    @pl.loop(1, NBETA)
    def _(d):
        beta_copy(vp, gz.at[b], sz_sem, gz_sem, d).start()

    @pl.loop(1, NALPHA)
    def _(d):
        alpha_copy(vp, ga.at[a], sa_sem, ga_sem, d).start()

    alpha_prepare()
    pl.loop(4, STEPS, unroll=4)(beta_step)

    @pl.loop(1, NALPHA)
    def _(d):
        alpha_copy(vp, ga.at[a], sa_sem, ga_sem, d).wait_recv()

    vh, vl = split(jnp.concatenate(
        [ga[:, 0:16, :].reshape(512, 128), unpack_tail(ga[:, 16:24, :]).reshape(512, 128)], axis=1))
    fh, fl = dot(a_oh_c[...], vh).astype(BF16), dot(a_oh_c[...], vl).astype(BF16)
    rh, rl = [], []
    for g in range(4):
        mine = slice(256 * g, 256 * g + 256)
        high, low = split(
            dot(a_kh[g], fh[mine]) + dot(a_kh[g], fl[mine]) + dot(a_kl[g], fh[mine]))
        rh.append(high)
        rl.append(low)
    rh, rl = jnp.concatenate(rh, 0), jnp.concatenate(rl, 0)
    asum = dot(a_oh_r[...], rh) + dot(a_oh_r[...], rl)
    ra_out[:, 0:16, :] = asum[:, 0:128].reshape(NALPHA, 16, 128)
    ra_out[:, 16:24, :] = pack_tail(asum[:, 128:256].reshape(NALPHA, 16, 128))

    @pl.loop(1, NALPHA)
    def _(d):
        alpha_copy(ra_out.at[alpha_peer(d)], ra_in.at[a], sra_sem, ra_sem, d).start()

    @pl.loop(1, NBETA)
    def _(d):
        beta_copy(vp, gz.at[b], sz_sem, gz_sem, d).wait_recv()

    for m in range(NBETA // 2):
        first, second = gz[2 * m], gz[2 * m + 1]
        turned = swap(second[0:16])
        za[:, 384 * m:384 * m + 128] = first[0:16]
        za[:, 384 * m + 128:384 * m + 256] = jnp.where(left_half, unpack_tail(first[16:24]), turned)
        za[:, 384 * m + 256:384 * m + 384] = jnp.where(
            left_half, turned, swap(unpack_tail(second[16:24])))
    for h in range(HIGH):
        high, low = split(za[:, LOW * h:LOW * (h + 1)])
        zsplit[32 * h:32 * h + 16, :] = high
        zsplit[32 * h + 16:32 * h + 32, :] = low
    acc[...] = jnp.zeros_like(acc)

    quarter = iota((1, 256), 1) >> 6

    def high_rows(step):
        return brow[pl.ds(pl.multiple_of(step * 8, 8), 8), :] >> 17

    def pair_row(rows, g):
        return jnp.concatenate([rows[2 * g:2 * g + 1, :], rows[2 * g + 1:2 * g + 2, :]], axis=1)

    @pl.loop(0, STEPS, unroll=6)
    def _(step):
        highs = high_rows(step)
        for g in range(4):
            at = pl.multiple_of(step * 1024 + 256 * g, 256)
            picked = dot(zsplit[...], b_oh_r[:, pl.ds(at, 256)])
            hrow = pair_row(highs, g)
            f = picked[0:32]
            for h in range(1, HIGH):
                f = jnp.where(hrow == h, picked[32 * h:32 * h + 32], f)
            fetched[:, pl.ds(at, 256)] = f.astype(BF16)

    @pl.loop(0, STEPS, unroll=6)
    def _(step):
        for g in range(4):
            at = pl.multiple_of(step * 1024 + 256 * g, 256)
            f = fetched[:, pl.ds(at, 256)].astype(F32)
            lhs = jnp.concatenate(
                [jnp.where(quarter == j, f, 0.0).astype(BF16) for j in range(4)], axis=0)
            back = dot(lhs, b_k[step * 4 + g])
            parts = []
            for j in (0, 2):
                h0, l0 = back[32 * j:32 * j + 16], back[32 * j + 16:32 * j + 32]
                h1, l1 = back[32 * j + 32:32 * j + 48], back[32 * j + 48:32 * j + 64]
                parts.append(jnp.where(left_half, h0 + l0, h1 + l1)
                             + pltpu.roll(jnp.where(left_half, h1, h0), 64, 1))
            r = jnp.concatenate(parts, 1)
            high, low = split(r)
            returned[0:16, pl.ds(at, 256)] = high
            returned[16:32, pl.ds(at, 256)] = low

    @pl.loop(0, STEPS, unroll=6)
    def _(step):
        highs = high_rows(step)
        lhs = []
        for g in range(4):
            at = pl.multiple_of(step * 1024 + 256 * g, 256)
            r = returned[:, pl.ds(at, 256)].astype(F32)
            hrow = pair_row(highs, g)
            lhs.append(jnp.concatenate(
                [jnp.where(hrow == h, r, 0.0).astype(BF16) for h in range(HIGH)], axis=0))
        at = pl.multiple_of(step * 1024, 1024)
        acc[...] += dot(jnp.concatenate(lhs, 1), b_oh_c[pl.ds(at, 1024), :])

    for h in range(HIGH):
        za[:, LOW * h:LOW * (h + 1)] = acc[32 * h:32 * h + 16, :] + acc[32 * h + 16:32 * h + 32, :]
    for m in range(NBETA // 2):
        t0 = za[:, 384 * m:384 * m + 128]
        t1 = za[:, 384 * m + 128:384 * m + 256]
        t2 = za[:, 384 * m + 256:384 * m + 384]
        rz_out[2 * m, 0:16] = t0
        rz_out[2 * m, 16:24] = pack_tail(t1)
        rz_out[2 * m + 1, 0:16] = swap(jnp.where(left_half, t2, t1))
        rz_out[2 * m + 1, 16:24] = pack_tail(swap(t2))

    @pl.loop(1, NBETA)
    def _(d):
        beta_copy(rz_out.at[beta_peer(d)], rz_in.at[b], srz_sem, rz_sem, d).start()

    ra_in[a] = ra_out[a]
    rz_in[b] = rz_out[b]

    @pl.loop(1, NALPHA)
    def _(d):
        alpha_copy(vp, ga.at[a], sa_sem, ga_sem, d).wait_send()
        alpha_copy(ra_out.at[alpha_peer(d)], ra_in.at[a], sra_sem, ra_sem, d).wait()

    total = ra_in[0]
    for i in range(1, NALPHA):
        total = total + ra_in[i]

    @pl.loop(1, NBETA)
    def _(d):
        beta_copy(vp, gz.at[b], sz_sem, gz_sem, d).wait_send()
        beta_copy(rz_out.at[beta_peer(d)], rz_in.at[b], srz_sem, rz_sem, d).wait()

    for i in range(NBETA):
        total = total + rz_in[i]
    out_ref[:, 0:128] = total[0:16]
    out_ref[:, 128:COLS] = unpack_tail(total[16:24])[:, 0:COLS - 128]


def local(vector, integrals, *lists):
    vmem = pl.BlockSpec(memory_space=pltpu.VMEM)
    hbm = pl.BlockSpec(memory_space=pltpu.HBM)
    dma = pltpu.SemaphoreType.DMA

    def block(*shape):
        return pltpu.VMEM(shape, F32)

    return pl.pallas_call(
        kernel,
        out_shape=jax.ShapeDtypeStruct((ROWS, COLS), F32),
        in_specs=[hbm] * 8,
        out_specs=vmem,
        scratch_shapes=[
            block(ROWS, COLS),
            block(ROWS, 256),
            block(24, 128),
            block(PAIRS, PAIRS),
            pltpu.VMEM((3, EXC, 128), I32),
            pltpu.VMEM((3, EXC, 384), I32),
            dma((8,)),
            block(256, 256),
            pltpu.VMEM((256, 256), BF16),
            pltpu.VMEM((256, 256), BF16),
            block(NALPHA, 24, 128),
            block(NBETA, 24, 128),
            block(ROWS, NBETA * COLS),
            pltpu.VMEM((2 * HIGH * ROWS, LOW), BF16),
            pltpu.VMEM((128, 128), I32),
            pltpu.VMEM((128, 128), I32),
            pltpu.VMEM((1024, NALPHA * ROWS), BF16),
            pltpu.VMEM((NALPHA * ROWS, 1024), BF16),
            pltpu.VMEM((4, 256, 256), BF16),
            pltpu.VMEM((4, 256, 256), BF16),
            pltpu.VMEM((128, 128), I32),
            pltpu.VMEM((128, 128), I32),
            pltpu.VMEM((ENTRIES, LOW), BF16),
            pltpu.VMEM((LOW, ENTRIES), BF16),
            pltpu.VMEM((TILES, 256, 128), BF16),
            pltpu.VMEM((2 * ROWS, ENTRIES), BF16),
            pltpu.VMEM((2 * ROWS, ENTRIES), BF16),
            block(2 * HIGH * ROWS, LOW),
            block(NALPHA, 24, 128),
            block(NALPHA, 24, 128),
            block(NBETA, 24, 128),
            block(NBETA, 24, 128),
            dma((NALPHA,)), dma((NALPHA,)), dma((NBETA,)), dma((NBETA,)),
            dma((NALPHA,)), dma((NALPHA,)), dma((NBETA,)), dma((NBETA,)),
        ],
        compiler_params=pltpu.CompilerParams(
            collective_id=0, has_side_effects=True, vmem_limit_bytes=54 * 1024 * 1024),
    )(vector, integrals, *lists)


def solution(mesh):
    placed = (P("alpha", "beta"), P(), P(), P(), P(), P(), P(), P())
    return jax.shard_map(
        local, mesh=mesh, in_specs=placed, out_specs=P("alpha", "beta"), check_vma=False
    )
```
